128 devices in a mesh: tm: 32 (over y_hi, x, z), col: 4 (over y_lo, core).
Axes of the slice: x: 4, y: 4 (y_hi: 2, y_lo: 2; y = y_hi * 2 + y_lo), z: 4, core: 2. Of those that a mesh axis runs over, the one named last changes fastest.
Arguments:
- design: float32 [16384, 32768], P('tm', 'col'), may hold values from -6 to 6
- fir_taps: float32 [128], replicated, may hold values from -0.5 to 0.5
- column_block: int32 [128], replicated, may hold values from 0 to 127, each once
- panels: int32 [2], replicated, may hold values from 0 to 127, as said below
Outputs:
- normal_rows: float32 [2, 256, 32768], P(None, 'tm', 'col')
The draws below stay inside these ranges and needn't reach their ends.
Inputs may be any that keep to these rules, and one draw needn't show every extreme that they name: column_block is a permutation of the block numbers. `panels`: the two entries differ; one of them is the last block number 128 - 1.
All inputs are finite; a program needn't handle non-finite values.
Results may differ from the reference program's by a relative error of at most 0.0001.
Values sent between devices are 32-bit elements; how exact they have to be, the bound alone decides.
No kernel may reach another device: no remote copies, remote signals or barrier semaphores. Data moves between devices by JAX's collectives and lax.ppermute only.
A program may use at most 128 MiB of HBM per device.

```python
import jax
import jax.numpy as jnp
from jax import lax

NCOL = 32768
PANEL = 256
TAPS = 128
EPOCHS = 16384
NBLK = 128


def draw_panels(key, part):
    block_total = NCOL // PANEL
    top_block = jnp.full((), block_total - 1, jnp.int32)
    other_block = jax.random.randint(jax.random.fold_in(key, 7), (), 0, block_total - 1).astype(jnp.int32)
    slot_pick = jax.random.randint(jax.random.fold_in(key, 11), (), 0, 2).astype(jnp.int32)
    first = jnp.where(slot_pick == 0, top_block, other_block)
    second = jnp.where(slot_pick == 0, other_block, top_block)
    return jnp.stack([first, second]).astype(jnp.int32)


def block_scale(own_key, shape, cuts, least, high):
    def one(dim, shards_of):
        heights = jax.random.uniform(jax.random.fold_in(jax.random.fold_in(own_key, 6), dim), (shards_of,), jnp.float32, least / len(cuts), high / len(cuts))
        return jnp.repeat(jnp.exp(heights), shape[dim] // shards_of).reshape((-1,) + (1,) * (len(shape) - dim - 1))

    factor_of = one(*cuts[0])
    for cut in cuts[1:]:
        factor_of = factor_of * one(*cut)
    return factor_of


def scatter_about(rng, shape, scale, most, split=(), kind=jnp.bfloat16):
    gain = block_scale(rng, shape, split, -0.22, 0.18) if split else 1.0
    entries = jax.random.normal(rng, shape, jnp.float32) * scale * gain
    return jnp.minimum(jnp.maximum(entries, -most), most).astype(kind)


def setup_inputs(seed: int = 0) -> dict:
    key_of = jax.random.split(jax.random.key(seed), 5)
    return {
        "design": scatter_about(key_of[0], (EPOCHS, NCOL), 1.0, 6.0, ((0, 32), (1, 4)), jnp.float32),
        "fir_taps": scatter_about(key_of[1], (TAPS,), TAPS ** -0.5, 0.5, (), jnp.float32),
        "column_block": jax.random.permutation(key_of[2], NCOL // PANEL).astype(jnp.int32),
        "panels": draw_panels(jax.random.fold_in(key_of[4], 71), 0),
    }


def fir_matrices(fir_taps):
    tap_count = fir_taps.shape[0]
    lag_index = jnp.arange(tap_count, dtype=jnp.int32)[:, None] - jnp.arange(tap_count, dtype=jnp.int32)[None, :]
    current = jnp.where(lag_index >= 0, fir_taps[jnp.clip(lag_index, 0, tap_count - 1)], jnp.zeros((), fir_taps.dtype))
    previous = jnp.where(lag_index < 0, fir_taps[jnp.clip(lag_index + tap_count, 0, tap_count - 1)], jnp.zeros((), fir_taps.dtype))
    return previous, current


def reference(design, fir_taps, column_block, panels):
    row_count, col_width = design.shape
    previous, current = fir_matrices(fir_taps)
    extended = jnp.concatenate([jnp.zeros((TAPS, col_width), design.dtype), design], axis=0)
    extended = extended.reshape(row_count // TAPS + 1, TAPS, col_width)
    filtered = jnp.einsum("rs,bsc->brc", previous, extended[:-1], precision=lax.Precision.HIGHEST, preferred_element_type=jnp.float32)
    filtered = filtered + jnp.einsum("rs,bsc->brc", current, extended[1:], precision=lax.Precision.HIGHEST, preferred_element_type=jnp.float32)
    filtered = filtered.reshape(row_count, col_width)
    block_ids = jnp.arange(NBLK, dtype=jnp.int32)
    results = []
    for panel_slot in range(2):
        target = panels[panel_slot]
        position = jnp.sum(jnp.where(column_block == target, block_ids, 0)).astype(jnp.int32)
        panel_cols = lax.dynamic_slice_in_dim(filtered, (position * PANEL).astype(jnp.int32), PANEL, 1)
        gram = lax.dot_general(panel_cols, filtered, (((0,), (0,)), ((), ())), precision=lax.Precision.HIGHEST, preferred_element_type=jnp.float32)
        upper_mask = jnp.repeat((column_block >= target).astype(jnp.float32), PANEL)
        results.append(gram * upper_mask[None, :] / EPOCHS)
    return jnp.stack(results, axis=0)
```

```python
import functools

import jax
import jax.numpy as jnp
import numpy as np
from jax import lax
from jax.experimental import pallas as pl
from jax.experimental.pallas import tpu as pltpu
from jax.sharding import Mesh
from jax.sharding import PartitionSpec as P

PANEL = 256
HALF = PANEL // 2
GROUP = 8
TM = ("y", "x", "z")
COL = ("yl", "core")
EVERY = (*TM, *COL)
SIZES = (3, 5, 7, 9, 11, 13, 15, 17)
CHAINS = 2
VMEM_LIMIT = 48 * 1024 * 1024
F32 = jnp.float32
I32 = jnp.int32

FLIPS = {"xa": 1 << 2, "xb": 3 << 2, "za": 1, "zb": 3, "y": 1 << 4}
ORDERS = (
    (("xa", "za", "xb", "zb", "y"), ("xb", "zb", "xa", "za", "y")),
    (("za", "xb", "zb", "xa", "y"), ("zb", "xa", "za", "xb", "y")),
)


def slot_flips(order):
    steps = len(order)
    return [
        functools.reduce(
            lambda a, k: a ^ (FLIPS[order[k]] if j >> (steps - 1 - k) & 1 else 0), range(steps), 0
        )
        for j in range(1 << steps)
    ]


def flip_pairs(chain, step):
    pairs = []
    for device in range(128):
        tm, col = device >> 2, device & 3
        flip = FLIPS[ORDERS[col & 1][chain][step]]
        pairs.append((device, (tm ^ flip) << 2 | col))
    return pairs


class Plan:
    def __init__(self, blocks):
        self.items = 0
        self.item_count = max(SIZES) * CHAINS
        self.place = self.item_count
        self.count = self.place + blocks
        self.diagonal = self.count + 1
        self.slot = self.diagonal + 1
        self.owner = self.slot + 1
        self.most = self.owner + 1
        self.last_block = self.most + 1
        self.size = 128


def plan_kernel(at, blocks, groups, block_ids, panels, coords, design, plan, pan, head, tail, sems):
    last = blocks * groups - 1
    low = panels[0] + panels[1] - last
    me = coords[0]
    plan[at.slot] = jnp.where(panels[0] == last, 1, 0).astype(I32)

    def local(k, carry):
        count, of_low, of_last = carry
        block = block_ids[me * blocks + k]
        active = block >= low
        plan[at.items + count] = k
        plan[at.place + k] = jnp.where(active, count, -1)
        return (
            count + active.astype(I32),
            jnp.where(block == low, k, of_low),
            jnp.where(block == last, k, of_last),
        )

    none = jnp.int32(-1)
    count, of_low, of_last = lax.fori_loop(0, blocks, local, (jnp.int32(0), none, none), unroll=8)
    low_at = jnp.maximum(of_low, 0) * PANEL
    last_at = jnp.maximum(of_last, 0) * PANEL
    rows, halo = pan.shape[0], head.shape[0]
    copies = []
    for slot, column in enumerate((low_at, last_at)):
        source = pl.ds(pl.multiple_of(column, PANEL), PANEL)
        target = pl.ds(slot * PANEL, PANEL)
        copies.append((design.at[pl.ds(rows - halo, halo), source], tail.at[:, target]))
        if slot == 0:
            copies.append((design.at[pl.ds(0, halo), source], head))
        copies.append((design.at[:, source], pan.at[:, target]))
    copies = [pltpu.make_async_copy(a, b, sems.at[i]) for i, (a, b) in enumerate(copies)]
    for copy in copies:
        copy.start()

    plan[at.items + count] = 0
    plan[at.count] = count
    plan[at.diagonal] = jnp.where(of_last >= 0, count, -1)
    plan[at.last_block] = jnp.maximum(of_last, 0)
    most = jnp.int32(0)
    owner = jnp.int32(0)
    for group in range(groups):

        def census(k, carry):
            count, owner = carry
            block = block_ids[group * blocks + k]
            count = count + (block >= low).astype(I32) + (block == last).astype(I32)
            return count, jnp.where(block == low, group, owner)

        count, owner = lax.fori_loop(0, blocks, census, (jnp.int32(0), owner), unroll=8)
        most = jnp.maximum(most, count)
    plan[at.owner] = owner
    plan[at.most] = most
    for copy in copies:
        copy.wait()


def make_plan(at, block_ids, panels, coords, design, blocks, groups, halo):
    rows = design.shape[0]
    smem = pl.BlockSpec(memory_space=pltpu.SMEM)
    vmem = pl.BlockSpec(memory_space=pltpu.VMEM)
    anywhere = pl.BlockSpec(memory_space=pl.ANY)
    return pl.pallas_call(
        functools.partial(plan_kernel, at, blocks, groups),
        out_shape=[
            jax.ShapeDtypeStruct((at.size,), I32),
            jax.ShapeDtypeStruct((rows, 2 * PANEL), F32),
            jax.ShapeDtypeStruct((halo, PANEL), F32),
            jax.ShapeDtypeStruct((halo, 2 * PANEL), F32),
        ],
        in_specs=[smem, smem, smem, anywhere],
        out_specs=[smem, vmem, vmem, vmem],
        scratch_shapes=[pltpu.SemaphoreType.DMA((5,))],
        compiler_params=pltpu.CompilerParams(vmem_limit_bytes=VMEM_LIMIT),
    )(block_ids, panels, coords, design)


def dot_exact(a, b):
    return jnp.dot(a, b, precision=lax.Precision.HIGHEST, preferred_element_type=F32)


def filter_kernel(scale, coords, taps, before, pan, after, own, other, square, double):
    tap_count = taps.shape[1]
    rows = pan.shape[0]
    blocks = rows // tap_count
    wide = jnp.broadcast_to(taps[...], (tap_count, tap_count))
    circulant = pltpu.roll(wide, 0, 1, stride=1, stride_axis=0)
    r = lax.broadcasted_iota(I32, circulant.shape, 0)
    s = lax.broadcasted_iota(I32, circulant.shape, 1)
    current = jnp.where(s >= r, circulant, 0.0)
    previous = jnp.where(s < r, circulant, 0.0)
    forward = jnp.concatenate([previous, current], axis=0)
    adjoint = jnp.concatenate([current.T, previous.T], axis=0) * scale
    columns = [before[...].T]
    columns += [pan[i * tap_count : (i + 1) * tap_count, :].T for i in range(blocks)]
    filtered = [
        dot_exact(jnp.concatenate(columns[i : i + 2], axis=1), forward) for i in range(blocks)
    ]
    of_last = jnp.concatenate([f[PANEL:] for f in filtered], axis=1)
    square[...] = scale * lax.dot_general(
        of_last,
        of_last,
        (((1,), (1,)), ((), ())),
        precision=lax.Precision.HIGHEST,
        preferred_element_type=F32,
    )
    filtered = [f[:PANEL] for f in filtered]
    beyond = jnp.concatenate([columns[-1][:PANEL], after[...].T], axis=1)
    at_end = coords[1] == coords[3] - 1
    filtered.append(jnp.where(at_end, 0.0, dot_exact(beyond, forward)))
    for i in range(blocks):
        both = jnp.concatenate(filtered[i : i + 2], axis=1)
        double[:, i * tap_count : (i + 1) * tap_count] = dot_exact(both, adjoint)
    core = coords[2]
    own[...] = double[pl.ds(pl.multiple_of(core * HALF, HALF), HALF), :]
    other[...] = double[pl.ds(pl.multiple_of((1 - core) * HALF, HALF), HALF), :]


def filter_twice(coords, taps, before, pan, after, epochs):
    rows = pan.shape[0]
    smem = pl.BlockSpec(memory_space=pltpu.SMEM)
    vmem = pl.BlockSpec(memory_space=pltpu.VMEM)
    return pl.pallas_call(
        functools.partial(filter_kernel, 1.0 / epochs),
        out_shape=[
            jax.ShapeDtypeStruct((HALF, rows), F32),
            jax.ShapeDtypeStruct((HALF, rows), F32),
            jax.ShapeDtypeStruct((PANEL, PANEL), F32),
        ],
        in_specs=[smem, vmem, vmem, vmem, vmem],
        out_specs=[vmem, vmem, vmem],
        scratch_shapes=[pltpu.VMEM((PANEL, rows), F32)],
        compiler_params=pltpu.CompilerParams(vmem_limit_bytes=VMEM_LIMIT),
    )(coords, taps, before, pan, after)


def product_kernel(at, plan, orders, own, other, square, design, *refs):
    outs = [refs[2 * chain : 2 * chain + 2] for chain in range(CHAINS)]
    held, whole, split, sems = refs[2 * CHAINS :]
    groups = PANEL // GROUP

    def fetch(item):
        block = pl.multiple_of(plan[at.items + item] * PANEL, PANEL)
        return pltpu.make_async_copy(design.at[:, pl.ds(block, PANEL)], held.at[item], sems.at[item])

    pairs = (plan[at.count] + 1) // CHAINS

    def start(item, carry):
        fetch(item).start()
        return carry

    lax.fori_loop(0, CHAINS * pairs, start, 0)
    core = orders[CHAINS * groups]
    whole[pl.ds(pl.multiple_of(core * HALF, HALF), HALF), :] = own[...]
    whole[pl.ds(pl.multiple_of((1 - core) * HALF, HALF), HALF), :] = other[...]
    for chain in range(CHAINS):
        for j in range(0, groups, 2):
            at_rows = [
                pl.ds(pl.multiple_of(orders[chain * groups + j + e] * GROUP, GROUP), GROUP)
                for e in range(2)
            ]
            rows = jnp.concatenate([whole[r, :] for r in at_rows], axis=0)
            top = rows.astype(jnp.bfloat16)
            split[chain, j * GROUP : (j + 2) * GROUP, :] = top
            rest = (rows - top.astype(F32)).astype(jnp.bfloat16)
            split[chain, PANEL + j * GROUP : PANEL + (j + 2) * GROUP, :] = rest

    dot = functools.partial(jnp.dot, preferred_element_type=F32)

    def multiply(pair, carry):
        for chain in range(CHAINS):
            item = CHAINS * pair + chain
            fetch(item).wait()
            block = held[item]
            top = block.astype(jnp.bfloat16)
            rest = (block - top.astype(F32)).astype(jnp.bfloat16)
            both = dot(split[chain], top)
            product = (both[PANEL:] + dot(split[chain, :PANEL, :], rest)) + both[:PANEL]
            for part, out in enumerate(outs[chain]):
                out[pair] = product[part * HALF : (part + 1) * HALF].reshape(out.shape[1:])
        return carry

    lax.fori_loop(0, pairs, multiply, 0)
    diagonal = plan[at.diagonal]
    for chain in range(CHAINS):

        @pl.when((diagonal >= 0) & (diagonal % CHAINS == chain))
        def _():
            for j in range(groups):
                row = pl.multiple_of(orders[chain * groups + j] * GROUP, GROUP)
                part, place = divmod(j, groups // 2)
                outs[chain][part][diagonal // CHAINS, place] = square[pl.ds(row, GROUP), :]


def products(at, size, plan, orders, own, other, square, design):
    rows = design.shape[0]
    out = jax.ShapeDtypeStruct((size, HALF // GROUP, GROUP, PANEL), F32)
    smem = pl.BlockSpec(memory_space=pltpu.SMEM)
    vmem = pl.BlockSpec(memory_space=pltpu.VMEM)
    return pl.pallas_call(
        functools.partial(product_kernel, at),
        out_shape=[out] * (2 * CHAINS),
        in_specs=[smem, smem, vmem, vmem, vmem, pl.BlockSpec(memory_space=pl.ANY)],
        out_specs=[vmem] * (2 * CHAINS),
        scratch_shapes=[
            pltpu.VMEM((CHAINS * size, rows, PANEL), F32),
            pltpu.VMEM((PANEL, rows), F32),
            pltpu.VMEM((CHAINS, 2 * PANEL, rows), jnp.bfloat16),
            pltpu.SemaphoreType.DMA((CHAINS * size,)),
        ],
        compiler_params=pltpu.CompilerParams(vmem_limit_bytes=VMEM_LIMIT),
        cost_estimate=pl.CostEstimate(
            flops=6 * CHAINS * size * rows * PANEL * PANEL,
            bytes_accessed=4 * CHAINS * size * PANEL * (rows + PANEL),
            transcendentals=0,
        ),
    )(plan, orders, own, other, square, design)


def place_kernel(at, blocks, plan, *refs):
    *parts, out, total = refs
    for chain in range(CHAINS):
        total[chain] = parts[2 * chain][:, 0] + parts[2 * chain + 1][:, 0]

    def item(index):
        return total[index % CHAINS, index // CHAINS]

    slot = plan[at.slot]
    for k in range(blocks):
        index = plan[at.place + k]
        found = item(jnp.maximum(index, 0))
        out[slot, :, k * PANEL : (k + 1) * PANEL] = jnp.where(index >= 0, found, 0.0)
    out[1 - slot] = jnp.zeros(out.shape[1:], F32)
    diagonal = plan[at.diagonal]

    @pl.when(diagonal >= 0)
    def _():
        column = pl.multiple_of(plan[at.last_block] * PANEL, PANEL)
        out[1 - slot, :, pl.ds(column, PANEL)] = item(diagonal)


def placed(at, plan, parts, blocks):
    size = parts[0].shape[0]
    smem = pl.BlockSpec(memory_space=pltpu.SMEM)
    vmem = pl.BlockSpec(memory_space=pltpu.VMEM)
    return pl.pallas_call(
        functools.partial(place_kernel, at, blocks),
        out_shape=jax.ShapeDtypeStruct((2, GROUP, blocks * PANEL), F32),
        in_specs=[smem] + [vmem] * len(parts),
        out_specs=vmem,
        scratch_shapes=[pltpu.VMEM((CHAINS, size, GROUP, PANEL), F32)],
    )(plan, *parts)


def rows_of(at, size, blocks, plan, orders, own, other, square, design):
    made = products(at, size, plan, orders, own, other, square, design)
    keeps, sends = list(made[::2]), list(made[1::2])
    for step in range(5):
        arrived = [
            lax.ppermute(sends[chain], EVERY, flip_pairs(chain, step)) for chain in range(CHAINS)
        ]
        if step < 4:
            half = keeps[0].shape[1] // 2
            sends = [k[:, half:] + a[:, half:] for k, a in zip(keeps, arrived)]
            keeps = [k[:, :half] + a[:, :half] for k, a in zip(keeps, arrived)]
    return placed(at, plan, [x for pair in zip(keeps, arrived) for x in pair], blocks)


def shards(design, fir_taps, column_block, panels):
    rows, width = design.shape
    halo = fir_taps.shape[0]
    blocks = width // PANEL
    groups = column_block.shape[0] // blocks
    shard_count = lax.axis_size(TM)
    tm, group = lax.axis_index(TM), lax.axis_index(COL)
    core, yl = lax.axis_index("core"), lax.axis_index("yl")
    at = Plan(blocks)
    coords = jnp.stack([group, tm, core, jnp.int32(shard_count)]).astype(I32)
    plan, pan, head, tail = make_plan(at, column_block, panels, coords, design, blocks, groups, halo)
    up = [(i, i + 1) for i in range(shard_count - 1)]
    down = [(i + 1, i) for i in range(shard_count - 1)]
    before = lax.ppermute(tail, TM, up)
    after = lax.ppermute(head, TM, down)
    own, other, square = filter_twice(
        coords, fir_taps.reshape(1, -1), before, pan, after, rows * shard_count
    )
    swap = [(0, 1), (1, 0)]
    owner = plan[at.owner]
    mine = jnp.where(owner == group, own, lax.ppermute(other, "core", swap))
    mine = jnp.where((owner >> 1) == yl, mine, lax.ppermute(mine, "yl", swap))
    other = lax.ppermute(mine, "core", swap)
    flips = [
        np.concatenate([np.array(slot_flips(order), np.int32) for order in ORDERS[c]])
        for c in range(2)
    ]
    orders = tm.astype(I32) ^ jnp.where(core == 0, flips[0], flips[1])
    orders = jnp.concatenate([orders, core.astype(I32)[None]])
    size_at = sum((plan[at.most] > CHAINS * size).astype(I32) for size in SIZES[:-1])
    branches = [
        functools.partial(rows_of, at, size, blocks) for size in SIZES
    ]
    return lax.switch(size_at, branches, plan, orders, mine, other, square, design)


def solution(mesh):
    finer = Mesh(mesh.devices.reshape(2, 4, 4, 2, 2), EVERY)
    return jax.shard_map(
        shards,
        mesh=finer,
        in_specs=(P(TM, COL), P(), P(), P()),
        out_specs=P(None, TM, COL),
        check_vma=False,
    )
```

```python
import functools

import jax
import jax.numpy as jnp
import numpy as np
from jax import lax
from jax.experimental import pallas as pl
from jax.experimental.pallas import tpu as pltpu
from jax.sharding import Mesh
from jax.sharding import PartitionSpec as P

PANEL = 256
HALF = PANEL // 2
GROUP = 8
TM = ("y", "x", "z")
COL = ("yl", "core")
EVERY = (*TM, *COL)
SIZES = (3, 5, 7, 9, 11, 13, 15, 17)
CHAINS = 2
MIB = 1024 * 1024
F32 = jnp.float32
I32 = jnp.int32

FLIPS = ((1, 3), (3, 1))
RING = 4


def halving_pairs(chain, step):
    pairs = []
    for device in range(128):
        ring_bits = 2 if device & 1 == 0 else 0
        pairs.append((device, device ^ FLIPS[chain][step] << 2 + ring_bits))
    return pairs


def shift_pairs(shift):
    pairs = []
    for device in range(128):
        ring_bits = 2 if device & 1 == 0 else 4
        place = device >> ring_bits & RING - 1
        moved = (place + shift) % RING
        pairs.append((device, device ^ (place ^ moved) << ring_bits))
    return pairs


def owners_of_slots(y, x, z, core):
    flips, shifts, ys = [], [], []
    for first, second in FLIPS:
        for j in range(32):
            flips.append((first if j >> 4 & 1 else 0) ^ (second if j >> 3 & 1 else 0))
            shifts.append(j >> 1 & RING - 1)
            ys.append(j & 1)
    flips, shifts, ys = (np.array(a, np.int32) for a in (flips, shifts, ys))
    flipped = jnp.where(core == 0, x, z) ^ flips
    shifted = (jnp.where(core == 0, z, x) + shifts) & (RING - 1)
    at_x = jnp.where(core == 0, flipped, shifted)
    at_z = jnp.where(core == 0, shifted, flipped)
    return ((y ^ ys) * RING + at_x) * RING + at_z


class Plan:
    def __init__(self, blocks):
        self.items = 0
        self.item_count = max(SIZES) * CHAINS
        self.place = self.item_count
        self.count = self.place + blocks
        self.diagonal = self.count + 1
        self.slot = self.diagonal + 1
        self.last_block = self.slot + 1
        self.size = 128


def plan_kernel(at, blocks, groups, block_ids, panels, coords, design, plan, choice, *refs):
    flags, pans, (head, tail, sems) = refs[:2], refs[2:4], refs[4:]
    last = blocks * groups - 1
    low = panels[0] + panels[1] - last
    me = coords[0]
    plan[at.slot] = jnp.where(panels[0] == last, 1, 0).astype(I32)

    def local(k, carry):
        count, of_low, of_last = carry
        block = block_ids[me * blocks + k]
        active = block >= low
        plan[at.items + count] = k
        plan[at.place + k] = jnp.where(active, count, -1)
        return (
            count + active.astype(I32),
            jnp.where(block == low, k, of_low),
            jnp.where(block == last, k, of_last),
        )

    none = jnp.int32(-1)
    count, of_low, of_last = lax.fori_loop(0, blocks, local, (jnp.int32(0), none, none), unroll=8)
    low_at = jnp.maximum(of_low, 0) * PANEL
    last_at = jnp.maximum(of_last, 0) * PANEL
    rows, halo = pans[0].shape[0], head.shape[0]
    copies = []
    for slot, column in enumerate((low_at, last_at)):
        source = pl.ds(pl.multiple_of(column, PANEL), PANEL)
        target = pl.ds(slot * PANEL, PANEL)
        copies.append((design.at[pl.ds(rows - halo, halo), source], tail.at[:, target]))
        if slot == 0:
            copies.append((design.at[pl.ds(0, halo), source], head))
        copies.append((design.at[:, source], pans[slot]))
    copies = [pltpu.make_async_copy(a, b, sems.at[i]) for i, (a, b) in enumerate(copies)]
    for copy in copies:
        copy.start()

    plan[at.items + count] = 0
    plan[at.count] = count
    plan[at.diagonal] = jnp.where(of_last >= 0, count, -1)
    plan[at.last_block] = jnp.maximum(of_last, 0)
    most = jnp.int32(0)
    owner = jnp.int32(0)
    for group in range(groups):

        def census(k, carry):
            count, owner = carry
            block = block_ids[group * blocks + k]
            count = count + (block >= low).astype(I32) + (block == last).astype(I32)
            return count, jnp.where(block == low, group, owner)

        count, owner = lax.fori_loop(0, blocks, census, (jnp.int32(0), owner), unroll=8)
        most = jnp.maximum(most, count)
    choice[0] = sum((most > CHAINS * size).astype(I32) for size in SIZES[:-1])
    for flag, truth in zip(flags, (owner == me, owner >> 1 == me >> 1)):
        flag[...] = jnp.full(flag.shape, truth.astype(I32), I32)
    for copy in copies:
        copy.wait()


def make_plan(at, block_ids, panels, coords, design, blocks, groups, halo):
    rows = design.shape[0]
    smem = pl.BlockSpec(memory_space=pltpu.SMEM)
    vmem = pl.BlockSpec(memory_space=pltpu.VMEM)
    anywhere = pl.BlockSpec(memory_space=pltpu.HBM)
    return pl.pallas_call(
        functools.partial(plan_kernel, at, blocks, groups),
        out_shape=[
            jax.ShapeDtypeStruct((at.size,), I32),
            jax.ShapeDtypeStruct((1,), I32),
            *[jax.ShapeDtypeStruct((1, rows), I32)] * 2,
            *[jax.ShapeDtypeStruct((rows, PANEL), F32)] * 2,
            jax.ShapeDtypeStruct((halo, PANEL), F32),
            jax.ShapeDtypeStruct((halo, 2 * PANEL), F32),
        ],
        in_specs=[smem, smem, smem, anywhere],
        out_specs=[smem] * 2 + [vmem] * 6,
        scratch_shapes=[pltpu.SemaphoreType.DMA((5,))],
        compiler_params=pltpu.CompilerParams(vmem_limit_bytes=46 * MIB),
    )(block_ids, panels, coords, design)


def dot_exact(a, b):
    return jnp.dot(a, b, precision=lax.Precision.HIGHEST, preferred_element_type=F32)


def tap_matrices(taps):
    tap_count = taps.shape[1]
    wide = jnp.broadcast_to(taps[...], (tap_count, tap_count))
    circulant = pltpu.roll(wide, 0, 1, stride=1, stride_axis=0)
    r = lax.broadcasted_iota(I32, circulant.shape, 0)
    s = lax.broadcasted_iota(I32, circulant.shape, 1)
    return jnp.where(s < r, circulant, 0.0), jnp.where(s >= r, circulant, 0.0)


def filter_kernel(scale, coords, taps, before, pan, after, own, other, columns, filtered, double):
    tap_count = taps.shape[1]
    rows = pan.shape[0]
    blocks = rows // tap_count
    previous, current = tap_matrices(taps)
    forward = jnp.concatenate([previous, current], axis=0)
    adjoint = jnp.concatenate([current.T, previous.T], axis=0) * scale
    columns[:, :tap_count] = before[:, :PANEL].T
    for i in range(blocks):
        at_rows = slice(i * tap_count, (i + 1) * tap_count)
        columns[:, (i + 1) * tap_count : (i + 2) * tap_count] = pan[at_rows, :].T
    columns[:, (blocks + 1) * tap_count :] = after[...].T

    def window(i, count):
        return pl.ds(pl.multiple_of(i * tap_count, tap_count), count * tap_count)

    def once(i, carry):
        filtered[:, window(i, 1)] = dot_exact(columns[:, window(i, 2)], forward)
        return carry

    def twice(i, carry):
        double[:, window(i, 1)] = dot_exact(filtered[:, window(i, 2)], adjoint)
        return carry

    lax.fori_loop(0, blocks + 1, once, 0)

    @pl.when(coords[1] == coords[3] - 1)
    def _():
        filtered[:, rows:] = jnp.zeros((PANEL, tap_count), F32)

    lax.fori_loop(0, blocks, twice, 0)
    core = coords[2]
    own[...] = double[pl.ds(pl.multiple_of(core * HALF, HALF), HALF), :]
    other[...] = double[pl.ds(pl.multiple_of((1 - core) * HALF, HALF), HALF), :]


def filter_twice(coords, taps, before, pan, after, epochs):
    rows = pan.shape[0]
    smem = pl.BlockSpec(memory_space=pltpu.SMEM)
    vmem = pl.BlockSpec(memory_space=pltpu.VMEM)
    return pl.pallas_call(
        functools.partial(filter_kernel, 1.0 / epochs),
        out_shape=[jax.ShapeDtypeStruct((HALF, rows), F32)] * 2,
        in_specs=[smem, vmem, vmem, vmem, vmem],
        out_specs=[vmem, vmem],
        scratch_shapes=[
            pltpu.VMEM((PANEL, rows + 2 * taps.size), F32),
            pltpu.VMEM((PANEL, rows + taps.size), F32),
            pltpu.VMEM((PANEL, rows), F32),
        ],
        compiler_params=pltpu.CompilerParams(vmem_limit_bytes=12 * MIB),
    )(coords, taps, before, pan, after)


def square_kernel(scale, taps, before, pan, square, held):
    tap_count = taps.shape[1]
    previous, current = tap_matrices(taps)
    backward = jnp.concatenate([previous.T, current.T], axis=1)
    held[:tap_count, :] = before[:, PANEL:]
    held[tap_count:, :] = pan[...]
    square[...] = jnp.zeros(square.shape, F32)

    def add(i, carry):
        both = held[pl.ds(pl.multiple_of(i * tap_count, tap_count), 2 * tap_count), :]
        filtered = dot_exact(backward, both)
        square[...] += scale * dot_exact(filtered.T, filtered)
        return carry

    lax.fori_loop(0, pan.shape[0] // tap_count, add, 0)


def filtered_square(taps, before, pan, epochs):
    vmem = pl.BlockSpec(memory_space=pltpu.VMEM)
    return pl.pallas_call(
        functools.partial(square_kernel, 1.0 / epochs),
        out_shape=jax.ShapeDtypeStruct((PANEL, PANEL), F32),
        in_specs=[vmem, vmem, vmem],
        out_specs=vmem,
        scratch_shapes=[pltpu.VMEM((pan.shape[0] + taps.size, PANEL), F32)],
        compiler_params=pltpu.CompilerParams(vmem_limit_bytes=8 * MIB),
        cost_estimate=pl.CostEstimate(
            flops=60 * pan.shape[0] * PANEL * PANEL, bytes_accessed=4 * pan.size, transcendentals=0
        ),
    )(taps, before, pan)


def product_kernel(at, plan, orders, own, other, square, design, *refs):
    outs = [refs[2 * chain : 2 * chain + 2] for chain in range(CHAINS)]
    whole, mixed, split, held, high, low, sems = refs[2 * CHAINS :]
    groups = PANEL // GROUP
    count = plan[at.count]

    def fetch(item):
        block = pl.multiple_of(plan[at.items + item] * PANEL, PANEL)
        return pltpu.make_async_copy(design.at[:, pl.ds(block, PANEL)], held.at[item], sems.at[item])

    def start(item, carry):
        fetch(item).start()
        return carry

    lax.fori_loop(0, count, start, 0)
    core = orders[CHAINS * groups]
    whole[pl.ds(pl.multiple_of(core * HALF, HALF), HALF), :] = own[...]
    whole[pl.ds(pl.multiple_of((1 - core) * HALF, HALF), HALF), :] = other[...]

    def rows_at(j):
        return pl.ds(pl.multiple_of(j * GROUP, GROUP), GROUP)

    def mix(j, carry):
        mixed[rows_at(j), :] = whole[rows_at(orders[j]), :]
        return carry

    lax.fori_loop(0, CHAINS * groups, mix, 0, unroll=4)
    for chain in range(CHAINS):
        rows = mixed[chain * PANEL : (chain + 1) * PANEL, :]
        top = rows.astype(jnp.bfloat16)
        split[chain, :PANEL, :] = top
        split[chain, PANEL:, :] = (rows - top.astype(F32)).astype(jnp.bfloat16)

    dot = functools.partial(jnp.dot, preferred_element_type=F32)

    def put(item, product):
        for chain in range(CHAINS):

            @pl.when(item % CHAINS == chain)
            def _():
                for part, out in enumerate(outs[chain]):
                    rows = product[part * HALF : (part + 1) * HALF]
                    out[item // CHAINS] = rows.reshape(out.shape[1:])

    def halve(item):
        block = held[item]
        top = block.astype(jnp.bfloat16)
        high[item % 2] = top
        low[item % 2] = (block - top.astype(F32)).astype(jnp.bfloat16)

    @pl.when(count > 0)
    def _():
        fetch(0).wait()
        halve(0)

    def multiply(item, carry):
        after = item + 1

        @pl.when(after < count)
        def _():
            fetch(after).wait()

        chain = item % CHAINS
        both = dot(split[chain], high[item % 2])
        rest = dot(split[chain, :PANEL, :], low[item % 2])
        halve(after)
        put(item, (both[PANEL:] + rest) + both[:PANEL])
        return carry

    lax.fori_loop(0, count, multiply, 0)
    diagonal = plan[at.diagonal]

    @pl.when(diagonal >= 0)
    def _():
        def move(j, carry):
            source = orders[diagonal % CHAINS * groups + j]
            mixed[rows_at(j), :PANEL] = square[rows_at(source), :]
            return carry

        lax.fori_loop(0, groups, move, 0)
        put(diagonal, mixed[:PANEL, :PANEL])


def products(at, size, plan, orders, own, other, square, design, blocks):
    rows = own.shape[1]
    out = jax.ShapeDtypeStruct((size, HALF // GROUP, GROUP, PANEL), F32)
    smem = pl.BlockSpec(memory_space=pltpu.SMEM)
    vmem = pl.BlockSpec(memory_space=pltpu.VMEM)
    return pl.pallas_call(
        functools.partial(product_kernel, at),
        out_shape=[out] * (2 * CHAINS),
        in_specs=[smem, smem] + [vmem] * 3 + [pl.BlockSpec(memory_space=pltpu.HBM)],
        out_specs=[vmem] * (2 * CHAINS),
        scratch_shapes=[
            pltpu.VMEM((PANEL, rows), F32),
            pltpu.VMEM((CHAINS * PANEL, rows), F32),
            pltpu.VMEM((CHAINS, 2 * PANEL, rows), jnp.bfloat16),
            pltpu.VMEM((blocks + 1, rows, PANEL), F32),
            pltpu.VMEM((2, rows, PANEL), jnp.bfloat16),
            pltpu.VMEM((2, rows, PANEL), jnp.bfloat16),
            pltpu.SemaphoreType.DMA((blocks,)),
        ],
        compiler_params=pltpu.CompilerParams(vmem_limit_bytes=44 * MIB),
        cost_estimate=pl.CostEstimate(
            flops=6 * CHAINS * size * rows * PANEL * PANEL,
            bytes_accessed=4 * CHAINS * size * PANEL * (rows + PANEL),
            transcendentals=0,
        ),
    )(plan, orders, own, other, square, design)


def place_kernel(at, blocks, plan, *refs):
    keep, arrived, out, total = refs
    size = total.shape[0] // CHAINS
    total[...] = keep[:, 0] + arrived[:, 0]

    def item(index):
        return total[index % CHAINS * size + index // CHAINS]

    slot = plan[at.slot]
    for k in range(blocks):
        index = plan[at.place + k]
        found = item(jnp.maximum(index, 0))
        out[slot, :, k * PANEL : (k + 1) * PANEL] = jnp.where(index >= 0, found, 0.0)
    out[1 - slot] = jnp.zeros(out.shape[1:], F32)
    diagonal = plan[at.diagonal]

    @pl.when(diagonal >= 0)
    def _():
        column = pl.multiple_of(plan[at.last_block] * PANEL, PANEL)
        out[1 - slot, :, pl.ds(column, PANEL)] = item(diagonal)


def placed(at, plan, parts, blocks):
    size = parts[0].shape[0]
    smem = pl.BlockSpec(memory_space=pltpu.SMEM)
    vmem = pl.BlockSpec(memory_space=pltpu.VMEM)
    return pl.pallas_call(
        functools.partial(place_kernel, at, blocks),
        out_shape=jax.ShapeDtypeStruct((2, GROUP, blocks * PANEL), F32),
        in_specs=[smem] + [vmem] * len(parts),
        out_specs=vmem,
        scratch_shapes=[pltpu.VMEM((size, GROUP, PANEL), F32)],
    )(plan, *parts)


def merge_kernel(*refs):
    sums, outs = refs[: 2 * CHAINS], refs[2 * CHAINS :]
    size = sums[0].shape[0]

    def merge(i, carry):
        for chain in range(CHAINS):
            keep, arrived = sums[2 * chain : 2 * chain + 2]
            for shift, out in enumerate(outs):
                for half in range(2):
                    row = 2 * shift + half
                    out[chain * size + i, half] = keep[i, row] + arrived[i, row]
        return carry

    lax.fori_loop(0, size, merge, 0)


def merged(keeps, arrived):
    size = keeps[0].shape[0]
    vmem = pl.BlockSpec(memory_space=pltpu.VMEM)
    out = jax.ShapeDtypeStruct((CHAINS * size, 2, GROUP, PANEL), F32)
    return pl.pallas_call(
        merge_kernel,
        out_shape=[out] * RING,
        in_specs=[vmem] * (2 * CHAINS),
        out_specs=[vmem] * RING,
        compiler_params=pltpu.CompilerParams(vmem_limit_bytes=24 * MIB),
    )(*[a for pair in zip(keeps, arrived) for a in pair])


def rows_of(at, size, blocks, plan, *made):
    made = [part[:size] for part in made]
    keeps, sends = made[::2], made[1::2]
    arrived = [lax.ppermute(sends[c], EVERY, halving_pairs(c, 0)) for c in range(CHAINS)]
    sends = [k[:, 8:] + a[:, 8:] for k, a in zip(keeps, arrived)]
    keeps = [k[:, :8] + a[:, :8] for k, a in zip(keeps, arrived)]
    arrived = [lax.ppermute(sends[c], EVERY, halving_pairs(c, 1)) for c in range(CHAINS)]
    total, *sends = merged(keeps, arrived)
    for shift in range(1, RING):
        total = total + lax.ppermute(sends[shift - 1], EVERY, shift_pairs(shift))
    keep, send = total[:, :1], total[:, 1:]
    arrived = lax.ppermute(send, "y", [(0, 1), (1, 0)])
    return placed(at, plan, [keep, arrived], blocks)


def shards(design, fir_taps, column_block, panels):
    rows, width = design.shape
    halo = fir_taps.shape[0]
    blocks = width // PANEL
    groups = column_block.shape[0] // blocks
    shard_count = lax.axis_size(TM)
    tm, group = lax.axis_index(TM), lax.axis_index(COL)
    core = lax.axis_index("core")
    at = Plan(blocks)
    coords = jnp.stack([group, tm, core, jnp.int32(shard_count)]).astype(I32)
    plan, choice, is_mine, on_chip, pan, last_pan, head, tail = make_plan(
        at, column_block, panels, coords, design, blocks, groups, halo
    )
    up = [(i, i + 1) for i in range(shard_count - 1)]
    down = [(i + 1, i) for i in range(shard_count - 1)]
    after = lax.ppermute(head, TM, down)
    before = lax.ppermute(tail, TM, up)
    taps = fir_taps.reshape(1, -1)
    epochs = rows * shard_count
    own, other = filter_twice(coords, taps, before, pan, after, epochs)
    swap = [(0, 1), (1, 0)]
    mine = jnp.where(is_mine > 0, own, lax.ppermute(other, "core", swap))
    last_pan, _ = lax.optimization_barrier((last_pan, mine))
    square = filtered_square(taps, before, last_pan, epochs)
    mine = jnp.where(on_chip > 0, mine, lax.ppermute(mine, "yl", swap))
    mine, square = lax.optimization_barrier((mine, square))
    other = lax.ppermute(mine, "core", swap)
    y, x, z = (lax.axis_index(a).astype(I32) for a in TM)
    orders = owners_of_slots(y, x, z, core.astype(I32))
    orders = jnp.concatenate([orders, core.astype(I32)[None]])
    made = products(at, max(SIZES), plan, orders, mine, other, square, design, blocks)
    branches = [functools.partial(rows_of, at, size, blocks) for size in SIZES]
    return lax.switch(choice[0], branches, plan, *made)


def solution(mesh):
    finer = Mesh(mesh.devices.reshape(2, 4, 4, 2, 2), EVERY)
    return jax.shard_map(
        shards,
        mesh=finer,
        in_specs=(P(TM, COL), P(), P(), P()),
        out_specs=P(None, TM, COL),
        check_vma=False,
    )
```

```python
import functools

import jax
import jax.numpy as jnp
import numpy as np
from jax import lax
from jax.experimental import pallas as pl
from jax.experimental.pallas import tpu as pltpu
from jax.sharding import Mesh
from jax.sharding import PartitionSpec as P

PANEL = 256
HALF = PANEL // 2
GROUP = 8
TM = ("y", "x", "z")
COL = ("yl", "core")
EVERY = (*TM, *COL)
SIZES = (3, 5, 7, 9, 11, 13, 15, 17)
CHAINS = 2
MIB = 1024 * 1024
F32 = jnp.float32
I32 = jnp.int32

FLIPS = ((1, 3), (3, 1))
RING = 4


def halving_pairs(chain, step):
    pairs = []
    for device in range(128):
        ring_bits = 2 if device & 1 == 0 else 0
        pairs.append((device, device ^ FLIPS[chain][step] << 2 + ring_bits))
    return pairs


def shift_pairs(shift):
    pairs = []
    for device in range(128):
        ring_bits = 2 if device & 1 == 0 else 4
        place = device >> ring_bits & RING - 1
        moved = (place + shift) % RING
        pairs.append((device, device ^ (place ^ moved) << ring_bits))
    return pairs


def owners_of_slots(y, x, z, core):
    flips, shifts, ys = [], [], []
    for first, second in FLIPS:
        for j in range(32):
            flips.append((first if j >> 4 & 1 else 0) ^ (second if j >> 3 & 1 else 0))
            shifts.append(j >> 1 & RING - 1)
            ys.append(j & 1)
    flips, shifts, ys = (np.array(a, np.int32) for a in (flips, shifts, ys))
    flipped = jnp.where(core == 0, x, z) ^ flips
    shifted = (jnp.where(core == 0, z, x) + shifts) & (RING - 1)
    at_x = jnp.where(core == 0, flipped, shifted)
    at_z = jnp.where(core == 0, shifted, flipped)
    return ((y ^ ys) * RING + at_x) * RING + at_z


class Plan:
    def __init__(self, blocks):
        self.items = 0
        self.item_count = max(SIZES) * CHAINS
        self.place = self.item_count
        self.count = self.place + blocks
        self.diagonal = self.count + 1
        self.slot = self.diagonal + 1
        self.last_block = self.slot + 1
        self.size = 128


def plan_kernel(at, blocks, groups, block_ids, panels, coords, design, plan, choice, *refs):
    flags, pans, edges, sems = refs[:2], refs[2:4], refs[4:6], refs[6]
    last = blocks * groups - 1
    low = panels[0] + panels[1] - last
    me = coords[0]
    plan[at.slot] = jnp.where(panels[0] == last, 1, 0).astype(I32)

    def local(k, carry):
        count, of_low, of_last = carry
        block = block_ids[me * blocks + k]
        active = block >= low
        plan[at.items + count] = k
        plan[at.place + k] = jnp.where(active, count, -1)
        return (
            count + active.astype(I32),
            jnp.where(block == low, k, of_low),
            jnp.where(block == last, k, of_last),
        )

    none = jnp.int32(-1)
    count, of_low, of_last = lax.fori_loop(0, blocks, local, (jnp.int32(0), none, none), unroll=8)
    low_at = jnp.maximum(of_low, 0) * PANEL
    last_at = jnp.maximum(of_last, 0) * PANEL
    rows, halo = pans[0].shape[0], edges[0].shape[0]
    odd = coords[1] % 2
    copies = []
    for slot, column in enumerate((low_at, last_at)):
        source = pl.ds(pl.multiple_of(column, PANEL), PANEL)
        target = pl.ds(slot * PANEL, PANEL)
        for edge, at_end in zip(edges, (1 - odd, odd)):
            first = pl.multiple_of(at_end * (rows - halo), GROUP)
            copies.append((design.at[pl.ds(first, halo), source], edge.at[:, target]))
        copies.append((design.at[:, source], pans[slot]))
    copies = [pltpu.make_async_copy(a, b, sems.at[i]) for i, (a, b) in enumerate(copies)]
    for copy in copies:
        copy.start()

    plan[at.items + count] = 0
    plan[at.count] = count
    plan[at.diagonal] = jnp.where(of_last >= 0, count, -1)
    plan[at.last_block] = jnp.maximum(of_last, 0)
    most = jnp.int32(0)
    owner = jnp.int32(0)
    for group in range(groups):

        def census(k, carry):
            count, owner = carry
            block = block_ids[group * blocks + k]
            count = count + (block >= low).astype(I32) + (block == last).astype(I32)
            return count, jnp.where(block == low, group, owner)

        count, owner = lax.fori_loop(0, blocks, census, (jnp.int32(0), owner), unroll=8)
        most = jnp.maximum(most, count)
    choice[0] = sum((most > CHAINS * size).astype(I32) for size in SIZES[:-1])
    for flag, truth in zip(flags, (owner == me, owner >> 1 == me >> 1)):
        flag[...] = jnp.full(flag.shape, truth.astype(I32), I32)
    for copy in copies:
        copy.wait()


def make_plan(at, block_ids, panels, coords, design, blocks, groups, halo):
    rows = design.shape[0]
    smem = pl.BlockSpec(memory_space=pltpu.SMEM)
    vmem = pl.BlockSpec(memory_space=pltpu.VMEM)
    anywhere = pl.BlockSpec(memory_space=pltpu.HBM)
    return pl.pallas_call(
        functools.partial(plan_kernel, at, blocks, groups),
        out_shape=[
            jax.ShapeDtypeStruct((at.size,), I32),
            jax.ShapeDtypeStruct((1,), I32),
            *[jax.ShapeDtypeStruct((1, rows), I32)] * 2,
            *[jax.ShapeDtypeStruct((rows, PANEL), F32)] * 2,
            *[jax.ShapeDtypeStruct((halo, 2 * PANEL), F32)] * 2,
        ],
        in_specs=[smem, smem, smem, anywhere],
        out_specs=[smem] * 2 + [vmem] * 6,
        scratch_shapes=[pltpu.SemaphoreType.DMA((6,))],
        compiler_params=pltpu.CompilerParams(vmem_limit_bytes=46 * MIB),
    )(block_ids, panels, coords, design)


def dot_exact(a, b):
    return jnp.dot(a, b, precision=lax.Precision.HIGHEST, preferred_element_type=F32)


def tap_matrices(taps):
    tap_count = taps.shape[1]
    wide = jnp.broadcast_to(taps[...], (tap_count, tap_count))
    circulant = pltpu.roll(wide, 0, 1, stride=1, stride_axis=0)
    r = lax.broadcasted_iota(I32, circulant.shape, 0)
    s = lax.broadcasted_iota(I32, circulant.shape, 1)
    return jnp.where(s < r, circulant, 0.0), jnp.where(s >= r, circulant, 0.0)


def filter_kernel(scale, coords, taps, pan, low_pair, high_pair, own, other, columns, filtered, double):
    tap_count = taps.shape[1]
    rows = pan.shape[0]
    blocks = rows // tap_count
    previous, current = tap_matrices(taps)
    forward = jnp.concatenate([previous, current], axis=0)
    adjoint = jnp.concatenate([current.T, previous.T], axis=0) * scale
    odd = coords[1] % 2 == 1
    columns[:, :tap_count] = jnp.where(odd, low_pair[:, :PANEL], high_pair[:, :PANEL]).T
    for i in range(blocks):
        at_rows = slice(i * tap_count, (i + 1) * tap_count)
        columns[:, (i + 1) * tap_count : (i + 2) * tap_count] = pan[at_rows, :].T
    after = jnp.where(odd, high_pair[:, :PANEL], low_pair[:, :PANEL])
    columns[:, (blocks + 1) * tap_count :] = after.T

    def window(i, count):
        return pl.ds(pl.multiple_of(i * tap_count, tap_count), count * tap_count)

    def once(i, carry):
        filtered[:, window(i, 1)] = dot_exact(columns[:, window(i, 2)], forward)
        return carry

    def twice(i, carry):
        double[:, window(i, 1)] = dot_exact(filtered[:, window(i, 2)], adjoint)
        return carry

    lax.fori_loop(0, blocks + 1, once, 0)

    @pl.when(coords[1] == coords[3] - 1)
    def _():
        filtered[:, rows:] = jnp.zeros((PANEL, tap_count), F32)

    lax.fori_loop(0, blocks, twice, 0)
    core = coords[2]
    own[...] = double[pl.ds(pl.multiple_of(core * HALF, HALF), HALF), :]
    other[...] = double[pl.ds(pl.multiple_of((1 - core) * HALF, HALF), HALF), :]


def filter_twice(coords, taps, pan, pairs, epochs):
    rows = pan.shape[0]
    smem = pl.BlockSpec(memory_space=pltpu.SMEM)
    vmem = pl.BlockSpec(memory_space=pltpu.VMEM)
    return pl.pallas_call(
        functools.partial(filter_kernel, 1.0 / epochs),
        out_shape=[jax.ShapeDtypeStruct((HALF, rows), F32)] * 2,
        in_specs=[smem, vmem, vmem, vmem, vmem],
        out_specs=[vmem, vmem],
        scratch_shapes=[
            pltpu.VMEM((PANEL, rows + 2 * taps.size), F32),
            pltpu.VMEM((PANEL, rows + taps.size), F32),
            pltpu.VMEM((PANEL, rows), F32),
        ],
        compiler_params=pltpu.CompilerParams(vmem_limit_bytes=12 * MIB),
    )(coords, taps, pan, *pairs)


def square_kernel(scale, coords, taps, pan, low_pair, high_pair, square, held):
    tap_count = taps.shape[1]
    previous, current = tap_matrices(taps)
    backward = jnp.concatenate([previous.T, current.T], axis=1)
    odd = coords[1] % 2 == 1
    held[:tap_count, :] = jnp.where(odd, low_pair[:, PANEL:], high_pair[:, PANEL:])
    held[tap_count:, :] = pan[...]
    square[...] = jnp.zeros(square.shape, F32)

    def add(i, carry):
        both = held[pl.ds(pl.multiple_of(i * tap_count, tap_count), 2 * tap_count), :]
        filtered = dot_exact(backward, both)
        square[...] += scale * dot_exact(filtered.T, filtered)
        return carry

    lax.fori_loop(0, pan.shape[0] // tap_count, add, 0)


def filtered_square(coords, taps, pan, pairs, epochs):
    smem = pl.BlockSpec(memory_space=pltpu.SMEM)
    vmem = pl.BlockSpec(memory_space=pltpu.VMEM)
    return pl.pallas_call(
        functools.partial(square_kernel, 1.0 / epochs),
        out_shape=jax.ShapeDtypeStruct((PANEL, PANEL), F32),
        in_specs=[smem] + [vmem] * 4,
        out_specs=vmem,
        scratch_shapes=[pltpu.VMEM((pan.shape[0] + taps.size, PANEL), F32)],
        compiler_params=pltpu.CompilerParams(vmem_limit_bytes=8 * MIB),
        cost_estimate=pl.CostEstimate(
            flops=60 * pan.shape[0] * PANEL * PANEL, bytes_accessed=4 * pan.size, transcendentals=0
        ),
    )(coords, taps, pan, *pairs)


def product_kernel(at, plan, orders, own, other, square, design, *refs):
    outs = [refs[2 * chain : 2 * chain + 2] for chain in range(CHAINS)]
    whole, mixed, split, held, high, low, sems = refs[2 * CHAINS :]
    groups = PANEL // GROUP
    count = plan[at.count]

    def fetch(item):
        block = pl.multiple_of(plan[at.items + item] * PANEL, PANEL)
        return pltpu.make_async_copy(design.at[:, pl.ds(block, PANEL)], held.at[item], sems.at[item])

    def start(item, carry):
        fetch(item).start()
        return carry

    lax.fori_loop(0, count, start, 0)
    core = orders[CHAINS * groups]
    whole[pl.ds(pl.multiple_of(core * HALF, HALF), HALF), :] = own[...]
    whole[pl.ds(pl.multiple_of((1 - core) * HALF, HALF), HALF), :] = other[...]

    def rows_at(j):
        return pl.ds(pl.multiple_of(j * GROUP, GROUP), GROUP)

    def mix(j, carry):
        mixed[rows_at(j), :] = whole[rows_at(orders[j]), :]
        return carry

    lax.fori_loop(0, CHAINS * groups, mix, 0, unroll=4)
    for chain in range(CHAINS):
        rows = mixed[chain * PANEL : (chain + 1) * PANEL, :]
        top = rows.astype(jnp.bfloat16)
        split[chain, :PANEL, :] = top
        split[chain, PANEL:, :] = (rows - top.astype(F32)).astype(jnp.bfloat16)

    dot = functools.partial(jnp.dot, preferred_element_type=F32)

    def put(item, product):
        for chain in range(CHAINS):

            @pl.when(item % CHAINS == chain)
            def _():
                for part, out in enumerate(outs[chain]):
                    rows = product[part * HALF : (part + 1) * HALF]
                    out[item // CHAINS] = rows.reshape(out.shape[1:])

    def halve(item):
        block = held[item]
        top = block.astype(jnp.bfloat16)
        high[item % 2] = top
        low[item % 2] = (block - top.astype(F32)).astype(jnp.bfloat16)

    @pl.when(count > 0)
    def _():
        fetch(0).wait()
        halve(0)

    def multiply(item, carry):
        after = item + 1

        @pl.when(after < count)
        def _():
            fetch(after).wait()

        chain = item % CHAINS
        both = dot(split[chain], high[item % 2])
        rest = dot(split[chain, :PANEL, :], low[item % 2])
        halve(after)
        put(item, (both[PANEL:] + rest) + both[:PANEL])
        return carry

    lax.fori_loop(0, count, multiply, 0)
    diagonal = plan[at.diagonal]

    @pl.when(diagonal >= 0)
    def _():
        def move(j, carry):
            source = orders[diagonal % CHAINS * groups + j]
            mixed[rows_at(j), :PANEL] = square[rows_at(source), :]
            return carry

        lax.fori_loop(0, groups, move, 0)
        put(diagonal, mixed[:PANEL, :PANEL])


def products(at, size, plan, orders, own, other, square, design, blocks):
    rows = own.shape[1]
    out = jax.ShapeDtypeStruct((size, HALF // GROUP, GROUP, PANEL), F32)
    smem = pl.BlockSpec(memory_space=pltpu.SMEM)
    vmem = pl.BlockSpec(memory_space=pltpu.VMEM)
    return pl.pallas_call(
        functools.partial(product_kernel, at),
        out_shape=[out] * (2 * CHAINS),
        in_specs=[smem, smem] + [vmem] * 3 + [pl.BlockSpec(memory_space=pltpu.HBM)],
        out_specs=[vmem] * (2 * CHAINS),
        scratch_shapes=[
            pltpu.VMEM((PANEL, rows), F32),
            pltpu.VMEM((CHAINS * PANEL, rows), F32),
            pltpu.VMEM((CHAINS, 2 * PANEL, rows), jnp.bfloat16),
            pltpu.VMEM((blocks + 1, rows, PANEL), F32),
            pltpu.VMEM((2, rows, PANEL), jnp.bfloat16),
            pltpu.VMEM((2, rows, PANEL), jnp.bfloat16),
            pltpu.SemaphoreType.DMA((blocks,)),
        ],
        compiler_params=pltpu.CompilerParams(vmem_limit_bytes=44 * MIB),
        cost_estimate=pl.CostEstimate(
            flops=6 * CHAINS * size * rows * PANEL * PANEL,
            bytes_accessed=4 * CHAINS * size * PANEL * (rows + PANEL),
            transcendentals=0,
        ),
    )(plan, orders, own, other, square, design)


def place_kernel(at, blocks, plan, *refs):
    keep, arrived, out, total = refs
    size = total.shape[0] // CHAINS
    total[...] = keep[:, 0] + arrived[:, 0]

    def item(index):
        return total[index % CHAINS * size + index // CHAINS]

    slot = plan[at.slot]
    for k in range(blocks):
        index = plan[at.place + k]
        found = item(jnp.maximum(index, 0))
        out[slot, :, k * PANEL : (k + 1) * PANEL] = jnp.where(index >= 0, found, 0.0)
    out[1 - slot] = jnp.zeros(out.shape[1:], F32)
    diagonal = plan[at.diagonal]

    @pl.when(diagonal >= 0)
    def _():
        column = pl.multiple_of(plan[at.last_block] * PANEL, PANEL)
        out[1 - slot, :, pl.ds(column, PANEL)] = item(diagonal)


def placed(at, plan, parts, blocks):
    size = parts[0].shape[0]
    smem = pl.BlockSpec(memory_space=pltpu.SMEM)
    vmem = pl.BlockSpec(memory_space=pltpu.VMEM)
    return pl.pallas_call(
        functools.partial(place_kernel, at, blocks),
        out_shape=jax.ShapeDtypeStruct((2, GROUP, blocks * PANEL), F32),
        in_specs=[smem] + [vmem] * len(parts),
        out_specs=vmem,
        scratch_shapes=[pltpu.VMEM((size, GROUP, PANEL), F32)],
        compiler_params=pltpu.CompilerParams(vmem_limit_bytes=8 * MIB),
    )(plan, *parts)


def merge_kernel(*refs):
    sums, outs = refs[: 2 * CHAINS], refs[2 * CHAINS :]
    size = sums[0].shape[0]

    def merge(i, carry):
        for chain in range(CHAINS):
            keep, arrived = sums[2 * chain : 2 * chain + 2]
            for shift, out in enumerate(outs):
                for half in range(2):
                    row = 2 * shift + half
                    out[chain * size + i, half] = keep[i, row] + arrived[i, row]
        return carry

    lax.fori_loop(0, size, merge, 0)


def merged(keeps, arrived):
    size = keeps[0].shape[0]
    vmem = pl.BlockSpec(memory_space=pltpu.VMEM)
    out = jax.ShapeDtypeStruct((CHAINS * size, 2, GROUP, PANEL), F32)
    return pl.pallas_call(
        merge_kernel,
        out_shape=[out] * RING,
        in_specs=[vmem] * (2 * CHAINS),
        out_specs=[vmem] * RING,
        compiler_params=pltpu.CompilerParams(vmem_limit_bytes=24 * MIB),
    )(*[a for pair in zip(keeps, arrived) for a in pair])


def rows_of(at, size, blocks, plan, *made):
    made = [part[:size] for part in made]
    keeps, sends = made[::2], made[1::2]
    arrived = [lax.ppermute(sends[c], EVERY, halving_pairs(c, 0)) for c in range(CHAINS)]
    sends = [k[:, 8:] + a[:, 8:] for k, a in zip(keeps, arrived)]
    keeps = [k[:, :8] + a[:, :8] for k, a in zip(keeps, arrived)]
    arrived = [lax.ppermute(sends[c], EVERY, halving_pairs(c, 1)) for c in range(CHAINS)]
    total, *sends = merged(keeps, arrived)
    for shift in range(1, RING):
        total = total + lax.ppermute(sends[shift - 1], EVERY, shift_pairs(shift))
    keep, send = total[:, :1], total[:, 1:]
    arrived = lax.ppermute(send, "y", [(0, 1), (1, 0)])
    return placed(at, plan, [keep, arrived], blocks)


def shards(design, fir_taps, column_block, panels):
    rows, width = design.shape
    halo = fir_taps.shape[0]
    blocks = width // PANEL
    groups = column_block.shape[0] // blocks
    shard_count = lax.axis_size(TM)
    tm, group = lax.axis_index(TM), lax.axis_index(COL)
    core = lax.axis_index("core")
    at = Plan(blocks)
    coords = jnp.stack([group, tm, core, jnp.int32(shard_count)]).astype(I32)
    plan, choice, is_mine, on_chip, pan, last_pan, *edges = make_plan(
        at, column_block, panels, coords, design, blocks, groups, halo
    )
    pairs = []
    for edge, first in zip(edges, (0, 1)):
        lower = range(first, shard_count - 1, 2)
        swaps = [(i, i + 1) for i in lower] + [(i + 1, i) for i in lower]
        pairs.append(lax.ppermute(edge, TM, swaps))
    taps = fir_taps.reshape(1, -1)
    epochs = rows * shard_count
    own, other = filter_twice(coords, taps, pan, pairs, epochs)
    swap = [(0, 1), (1, 0)]
    mine = jnp.where(is_mine > 0, own, lax.ppermute(other, "core", swap))
    last_pan, _ = lax.optimization_barrier((last_pan, mine))
    square = filtered_square(coords, taps, last_pan, pairs, epochs)
    mine = jnp.where(on_chip > 0, mine, lax.ppermute(mine, "yl", swap))
    mine, square = lax.optimization_barrier((mine, square))
    other = lax.ppermute(mine, "core", swap)
    y, x, z = (lax.axis_index(a).astype(I32) for a in TM)
    orders = owners_of_slots(y, x, z, core.astype(I32))
    orders = jnp.concatenate([orders, core.astype(I32)[None]])
    made = products(at, max(SIZES), plan, orders, mine, other, square, design, blocks)
    branches = [functools.partial(rows_of, at, size, blocks) for size in SIZES]
    return lax.switch(choice[0], branches, plan, *made)


def solution(mesh):
    finer = Mesh(mesh.devices.reshape(2, 4, 4, 2, 2), EVERY)
    return jax.shard_map(
        shards,
        mesh=finer,
        in_specs=(P(TM, COL), P(), P(), P()),
        out_specs=P(None, TM, COL),
        check_vma=False,
    )
```

```python
import functools

import jax
import jax.numpy as jnp
import numpy as np
from jax import lax
from jax.experimental import pallas as pl
from jax.experimental.pallas import tpu as pltpu
from jax.sharding import Mesh
from jax.sharding import PartitionSpec as P

PANEL = 256
HALF = PANEL // 2
GROUP = 8
TM = ("y", "x", "z")
COL = ("yl", "core")
EVERY = (*TM, *COL)
SIZES = (3, 5, 7, 9, 11, 13, 15, 17)
CHAINS = 2
MIB = 1024 * 1024
F32 = jnp.float32
I32 = jnp.int32

FLIPS = ((1, 3), (3, 1))
RING = 4


def halving_pairs(chain, step):
    pairs = []
    for device in range(128):
        ring_bits = 2 if device & 1 == 0 else 0
        pairs.append((device, device ^ FLIPS[chain][step] << 2 + ring_bits))
    return pairs


def shift_pairs(shift):
    pairs = []
    for device in range(128):
        ring_bits = 2 if device & 1 == 0 else 4
        place = device >> ring_bits & RING - 1
        moved = (place + shift) % RING
        pairs.append((device, device ^ (place ^ moved) << ring_bits))
    return pairs


def owners_of_slots(y, x, z, core):
    flips, shifts, ys = [], [], []
    for first, second in FLIPS:
        for j in range(32):
            flips.append((first if j >> 4 & 1 else 0) ^ (second if j >> 3 & 1 else 0))
            shifts.append(j >> 1 & RING - 1)
            ys.append(j & 1)
    flips, shifts, ys = (np.array(a, np.int32) for a in (flips, shifts, ys))
    flipped = jnp.where(core == 0, x, z) ^ flips
    shifted = (jnp.where(core == 0, z, x) + shifts) & (RING - 1)
    at_x = jnp.where(core == 0, flipped, shifted)
    at_z = jnp.where(core == 0, shifted, flipped)
    return ((y ^ ys) * RING + at_x) * RING + at_z


class Plan:
    def __init__(self, blocks):
        self.items = 0
        self.item_count = max(SIZES) * CHAINS
        self.place = self.item_count
        self.count = self.place + blocks
        self.diagonal = self.count + 1
        self.slot = self.diagonal + 1
        self.last_block = self.slot + 1
        self.size = 128


def plan_kernel(at, blocks, groups, block_ids, panels, coords, design, plan, choice, *refs):
    flags, pans, edges, sems = refs[:2], refs[2:4], refs[4:6], refs[6]
    last = blocks * groups - 1
    low = panels[0] + panels[1] - last
    me = coords[0]
    plan[at.slot] = jnp.where(panels[0] == last, 1, 0).astype(I32)

    def local(k, carry):
        count, of_low, of_last = carry
        block = block_ids[me * blocks + k]
        active = block >= low
        plan[at.items + count] = k
        plan[at.place + k] = jnp.where(active, count, -1)
        return (
            count + active.astype(I32),
            jnp.where(block == low, k, of_low),
            jnp.where(block == last, k, of_last),
        )

    none = jnp.int32(-1)
    count, of_low, of_last = lax.fori_loop(0, blocks, local, (jnp.int32(0), none, none), unroll=8)
    low_at = jnp.maximum(of_low, 0) * PANEL
    last_at = jnp.maximum(of_last, 0) * PANEL
    rows, halo = pans[0].shape[0], edges[0].shape[0]
    odd = coords[1] % 2
    copies = []
    for slot, column in enumerate((low_at, last_at)):
        source = pl.ds(pl.multiple_of(column, PANEL), PANEL)
        target = pl.ds(slot * PANEL, PANEL)
        for edge, at_end in zip(edges, (1 - odd, odd)):
            first = pl.multiple_of(at_end * (rows - halo), GROUP)
            copies.append((design.at[pl.ds(first, halo), source], edge.at[:, target]))
        copies.append((design.at[:, source], pans[slot]))
    copies = [pltpu.make_async_copy(a, b, sems.at[i]) for i, (a, b) in enumerate(copies)]
    for copy in copies:
        copy.start()

    plan[at.items + count] = 0
    plan[at.count] = count
    plan[at.diagonal] = jnp.where(of_last >= 0, count, -1)
    plan[at.last_block] = jnp.maximum(of_last, 0)
    most = jnp.int32(0)
    owner = jnp.int32(0)
    for group in range(groups):

        def census(k, carry):
            count, owner = carry
            block = block_ids[group * blocks + k]
            count = count + (block >= low).astype(I32) + (block == last).astype(I32)
            return count, jnp.where(block == low, group, owner)

        count, owner = lax.fori_loop(0, blocks, census, (jnp.int32(0), owner), unroll=8)
        most = jnp.maximum(most, count)
    choice[0] = sum((most > CHAINS * size).astype(I32) for size in SIZES[:-1])
    for flag, truth in zip(flags, (owner == me, owner >> 1 == me >> 1)):
        flag[...] = jnp.full(flag.shape, truth.astype(I32), I32)
    for copy in copies:
        copy.wait()


def make_plan(at, block_ids, panels, coords, design, blocks, groups, halo):
    rows = design.shape[0]
    smem = pl.BlockSpec(memory_space=pltpu.SMEM)
    vmem = pl.BlockSpec(memory_space=pltpu.VMEM)
    anywhere = pl.BlockSpec(memory_space=pltpu.HBM)
    return pl.pallas_call(
        functools.partial(plan_kernel, at, blocks, groups),
        out_shape=[
            jax.ShapeDtypeStruct((at.size,), I32),
            jax.ShapeDtypeStruct((1,), I32),
            *[jax.ShapeDtypeStruct((1, rows), I32)] * 2,
            *[jax.ShapeDtypeStruct((rows, PANEL), F32)] * 2,
            *[jax.ShapeDtypeStruct((halo, 2 * PANEL), F32)] * 2,
        ],
        in_specs=[smem, smem, smem, anywhere],
        out_specs=[smem] * 2 + [vmem] * 6,
        scratch_shapes=[pltpu.SemaphoreType.DMA((6,))],
        compiler_params=pltpu.CompilerParams(vmem_limit_bytes=46 * MIB),
    )(block_ids, panels, coords, design)


def dot_exact(a, b):
    return jnp.dot(a, b, precision=lax.Precision.HIGHEST, preferred_element_type=F32)


def tap_matrices(taps):
    tap_count = taps.shape[1]
    wide = jnp.broadcast_to(taps[...], (tap_count, tap_count))
    circulant = pltpu.roll(wide, 0, 1, stride=1, stride_axis=0)
    r = lax.broadcasted_iota(I32, circulant.shape, 0)
    s = lax.broadcasted_iota(I32, circulant.shape, 1)
    return jnp.where(s < r, circulant, 0.0), jnp.where(s >= r, circulant, 0.0)


def filter_kernel(scale, coords, taps, pan, low_pair, high_pair, own, other, columns, filtered, double):
    tap_count = taps.shape[1]
    rows = pan.shape[0]
    blocks = rows // tap_count
    previous, current = tap_matrices(taps)
    forward = jnp.concatenate([previous, current], axis=0)
    adjoint = jnp.concatenate([current.T, previous.T], axis=0) * scale
    odd = coords[1] % 2 == 1
    columns[:, :tap_count] = jnp.where(odd, low_pair[:, :PANEL], high_pair[:, :PANEL]).T
    for i in range(blocks):
        at_rows = slice(i * tap_count, (i + 1) * tap_count)
        columns[:, (i + 1) * tap_count : (i + 2) * tap_count] = pan[at_rows, :].T
    after = jnp.where(odd, high_pair[:, :PANEL], low_pair[:, :PANEL])
    columns[:, (blocks + 1) * tap_count :] = after.T

    def window(i, count):
        return pl.ds(pl.multiple_of(i * tap_count, tap_count), count * tap_count)

    def once(i, carry):
        filtered[:, window(i, 1)] = dot_exact(columns[:, window(i, 2)], forward)
        return carry

    def twice(i, carry):
        double[:, window(i, 1)] = dot_exact(filtered[:, window(i, 2)], adjoint)
        return carry

    lax.fori_loop(0, blocks + 1, once, 0)

    @pl.when(coords[1] == coords[3] - 1)
    def _():
        filtered[:, rows:] = jnp.zeros((PANEL, tap_count), F32)

    lax.fori_loop(0, blocks, twice, 0)
    core = coords[2]
    own[...] = double[pl.ds(pl.multiple_of(core * HALF, HALF), HALF), :]
    other[...] = double[pl.ds(pl.multiple_of((1 - core) * HALF, HALF), HALF), :]


def filter_twice(coords, taps, pan, pairs, epochs):
    rows = pan.shape[0]
    smem = pl.BlockSpec(memory_space=pltpu.SMEM)
    vmem = pl.BlockSpec(memory_space=pltpu.VMEM)
    return pl.pallas_call(
        functools.partial(filter_kernel, 1.0 / epochs),
        out_shape=[jax.ShapeDtypeStruct((HALF, rows), F32)] * 2,
        in_specs=[smem, vmem, vmem, vmem, vmem],
        out_specs=[vmem, vmem],
        scratch_shapes=[
            pltpu.VMEM((PANEL, rows + 2 * taps.size), F32),
            pltpu.VMEM((PANEL, rows + taps.size), F32),
            pltpu.VMEM((PANEL, rows), F32),
        ],
        compiler_params=pltpu.CompilerParams(vmem_limit_bytes=12 * MIB),
    )(coords, taps, pan, *pairs)


def square_kernel(scale, coords, taps, pan, low_pair, high_pair, square, held):
    tap_count = taps.shape[1]
    previous, current = tap_matrices(taps)
    backward = jnp.concatenate([previous.T, current.T], axis=1)
    odd = coords[1] % 2 == 1
    held[:tap_count, :] = jnp.where(odd, low_pair[:, PANEL:], high_pair[:, PANEL:])
    held[tap_count:, :] = pan[...]
    square[...] = jnp.zeros(square.shape, F32)

    def add(i, carry):
        both = held[pl.ds(pl.multiple_of(i * tap_count, tap_count), 2 * tap_count), :]
        filtered = dot_exact(backward, both)
        square[...] += scale * dot_exact(filtered.T, filtered)
        return carry

    lax.fori_loop(0, pan.shape[0] // tap_count, add, 0)


def filtered_square(coords, taps, pan, pairs, epochs):
    smem = pl.BlockSpec(memory_space=pltpu.SMEM)
    vmem = pl.BlockSpec(memory_space=pltpu.VMEM)
    return pl.pallas_call(
        functools.partial(square_kernel, 1.0 / epochs),
        out_shape=jax.ShapeDtypeStruct((PANEL, PANEL), F32),
        in_specs=[smem] + [vmem] * 4,
        out_specs=vmem,
        scratch_shapes=[pltpu.VMEM((pan.shape[0] + taps.size, PANEL), F32)],
        compiler_params=pltpu.CompilerParams(vmem_limit_bytes=8 * MIB),
        cost_estimate=pl.CostEstimate(
            flops=60 * pan.shape[0] * PANEL * PANEL, bytes_accessed=4 * pan.size, transcendentals=0
        ),
    )(coords, taps, pan, *pairs)


def product_kernel(at, plan, orders, own, other, square, design, *refs):
    outs = [refs[2 * chain : 2 * chain + 2] for chain in range(CHAINS)]
    whole, mixed, split, held, high, low, sems = refs[2 * CHAINS :]
    groups = PANEL // GROUP
    count = plan[at.count]

    def fetch(item):
        block = pl.multiple_of(plan[at.items + item] * PANEL, PANEL)
        return pltpu.make_async_copy(design.at[:, pl.ds(block, PANEL)], held.at[item], sems.at[item])

    def start(item, carry):
        fetch(item).start()
        return carry

    lax.fori_loop(0, count, start, 0)
    core = orders[CHAINS * groups]
    whole[pl.ds(pl.multiple_of(core * HALF, HALF), HALF), :] = own[...]
    whole[pl.ds(pl.multiple_of((1 - core) * HALF, HALF), HALF), :] = other[...]

    def rows_at(j):
        return pl.ds(pl.multiple_of(j * GROUP, GROUP), GROUP)

    def mix(j, carry):
        mixed[rows_at(j), :] = whole[rows_at(orders[j]), :]
        return carry

    lax.fori_loop(0, CHAINS * groups, mix, 0, unroll=4)
    for chain in range(CHAINS):
        rows = mixed[chain * PANEL : (chain + 1) * PANEL, :]
        top = rows.astype(jnp.bfloat16)
        split[chain, :PANEL, :] = top
        split[chain, PANEL:, :] = (rows - top.astype(F32)).astype(jnp.bfloat16)

    dot = functools.partial(jnp.dot, preferred_element_type=F32)

    def put(item, product):
        for chain in range(CHAINS):

            @pl.when(item % CHAINS == chain)
            def _():
                for part, out in enumerate(outs[chain]):
                    rows = product[part * HALF : (part + 1) * HALF]
                    out[item // CHAINS] = rows.reshape(out.shape[1:])

    def halve(item):
        block = held[item]
        top = block.astype(jnp.bfloat16)
        high[item % 2] = top
        low[item % 2] = (block - top.astype(F32)).astype(jnp.bfloat16)

    @pl.when(count > 0)
    def _():
        fetch(0).wait()
        halve(0)

    def multiply(item, carry):
        after = item + 1

        @pl.when(after < count)
        def _():
            fetch(after).wait()

        chain = item % CHAINS
        both = dot(split[chain], high[item % 2])
        rest = dot(split[chain, :PANEL, :], low[item % 2])
        halve(after)
        put(item, (both[PANEL:] + rest) + both[:PANEL])
        return carry

    lax.fori_loop(0, count, multiply, 0)
    diagonal = plan[at.diagonal]

    @pl.when(diagonal >= 0)
    def _():
        def move(j, carry):
            source = orders[diagonal % CHAINS * groups + j]
            mixed[rows_at(j), :PANEL] = square[rows_at(source), :]
            return carry

        lax.fori_loop(0, groups, move, 0)
        put(diagonal, mixed[:PANEL, :PANEL])


def products(at, size, plan, orders, own, other, square, design, blocks):
    rows = own.shape[1]
    out = jax.ShapeDtypeStruct((size, HALF // GROUP, GROUP, PANEL), F32)
    smem = pl.BlockSpec(memory_space=pltpu.SMEM)
    vmem = pl.BlockSpec(memory_space=pltpu.VMEM)
    return pl.pallas_call(
        functools.partial(product_kernel, at),
        out_shape=[out] * (2 * CHAINS),
        in_specs=[smem, smem] + [vmem] * 3 + [pl.BlockSpec(memory_space=pltpu.HBM)],
        out_specs=[vmem] * (2 * CHAINS),
        scratch_shapes=[
            pltpu.VMEM((PANEL, rows), F32),
            pltpu.VMEM((CHAINS * PANEL, rows), F32),
            pltpu.VMEM((CHAINS, 2 * PANEL, rows), jnp.bfloat16),
            pltpu.VMEM((blocks + 1, rows, PANEL), F32),
            pltpu.VMEM((2, rows, PANEL), jnp.bfloat16),
            pltpu.VMEM((2, rows, PANEL), jnp.bfloat16),
            pltpu.SemaphoreType.DMA((blocks,)),
        ],
        compiler_params=pltpu.CompilerParams(vmem_limit_bytes=44 * MIB),
        cost_estimate=pl.CostEstimate(
            flops=6 * CHAINS * size * rows * PANEL * PANEL,
            bytes_accessed=4 * CHAINS * size * PANEL * (rows + PANEL),
            transcendentals=0,
        ),
    )(plan, orders, own, other, square, design)


def place_kernel(at, blocks, plan, *refs):
    keep, arrived, out, total = refs
    size = total.shape[0] // CHAINS
    total[...] = keep[:, 0] + arrived[:, 0]

    def item(index):
        return total[index % CHAINS * size + index // CHAINS]

    slot = plan[at.slot]
    for k in range(blocks):
        index = plan[at.place + k]
        found = item(jnp.maximum(index, 0))
        out[slot, :, k * PANEL : (k + 1) * PANEL] = jnp.where(index >= 0, found, 0.0)
    out[1 - slot] = jnp.zeros(out.shape[1:], F32)
    diagonal = plan[at.diagonal]

    @pl.when(diagonal >= 0)
    def _():
        column = pl.multiple_of(plan[at.last_block] * PANEL, PANEL)
        out[1 - slot, :, pl.ds(column, PANEL)] = item(diagonal)


def placed(at, plan, parts, blocks):
    size = parts[0].shape[0]
    smem = pl.BlockSpec(memory_space=pltpu.SMEM)
    vmem = pl.BlockSpec(memory_space=pltpu.VMEM)
    return pl.pallas_call(
        functools.partial(place_kernel, at, blocks),
        out_shape=jax.ShapeDtypeStruct((2, GROUP, blocks * PANEL), F32),
        in_specs=[smem] + [vmem] * len(parts),
        out_specs=vmem,
        scratch_shapes=[pltpu.VMEM((size, GROUP, PANEL), F32)],
        compiler_params=pltpu.CompilerParams(vmem_limit_bytes=8 * MIB),
    )(plan, *parts)


def merge_kernel(*refs):
    sums, outs = refs[: 2 * CHAINS], refs[2 * CHAINS :]
    size = sums[0].shape[0]

    def merge(i, carry):
        for chain in range(CHAINS):
            keep, arrived = sums[2 * chain : 2 * chain + 2]
            for shift, out in enumerate(outs):
                for half in range(2):
                    row = 2 * shift + half
                    out[chain * size + i, half] = keep[i, row] + arrived[i, row]
        return carry

    lax.fori_loop(0, size, merge, 0)


def merged(keeps, arrived):
    size = keeps[0].shape[0]
    vmem = pl.BlockSpec(memory_space=pltpu.VMEM)
    out = jax.ShapeDtypeStruct((CHAINS * size, 2, GROUP, PANEL), F32)
    return pl.pallas_call(
        merge_kernel,
        out_shape=[out] * RING,
        in_specs=[vmem] * (2 * CHAINS),
        out_specs=[vmem] * RING,
        compiler_params=pltpu.CompilerParams(vmem_limit_bytes=24 * MIB),
    )(*[a for pair in zip(keeps, arrived) for a in pair])


def rows_of(at, size, blocks, plan, *made):
    made = [part[:size] for part in made]
    keeps, sends = made[::2], made[1::2]
    arrived = [lax.ppermute(sends[c], EVERY, halving_pairs(c, 0)) for c in range(CHAINS)]
    sends = [k[:, 8:] + a[:, 8:] for k, a in zip(keeps, arrived)]
    keeps = [k[:, :8] + a[:, :8] for k, a in zip(keeps, arrived)]
    arrived = [lax.ppermute(sends[c], EVERY, halving_pairs(c, 1)) for c in range(CHAINS)]
    total, *sends = merged(keeps, arrived)
    for shift in (2, 1, 3):
        total = total + lax.ppermute(sends[shift - 1], EVERY, shift_pairs(shift))
    keep, send = total[:, :1], total[:, 1:]
    arrived = lax.ppermute(send, "y", [(0, 1), (1, 0)])
    return placed(at, plan, [keep, arrived], blocks)


def shards(design, fir_taps, column_block, panels):
    rows, width = design.shape
    halo = fir_taps.shape[0]
    blocks = width // PANEL
    groups = column_block.shape[0] // blocks
    shard_count = lax.axis_size(TM)
    tm, group = lax.axis_index(TM), lax.axis_index(COL)
    core = lax.axis_index("core")
    at = Plan(blocks)
    coords = jnp.stack([group, tm, core, jnp.int32(shard_count)]).astype(I32)
    plan, choice, is_mine, on_chip, pan, last_pan, *edges = make_plan(
        at, column_block, panels, coords, design, blocks, groups, halo
    )
    pairs = []
    for edge, first in zip(edges, (0, 1)):
        lower = range(first, shard_count - 1, 2)
        swaps = [(i, i + 1) for i in lower] + [(i + 1, i) for i in lower]
        pairs.append(lax.ppermute(edge, TM, swaps))
    taps = fir_taps.reshape(1, -1)
    epochs = rows * shard_count
    own, other = filter_twice(coords, taps, pan, pairs, epochs)
    swap = [(0, 1), (1, 0)]
    mine = jnp.where(is_mine > 0, own, lax.ppermute(other, "core", swap))
    last_pan, _ = lax.optimization_barrier((last_pan, mine))
    square = filtered_square(coords, taps, last_pan, pairs, epochs)
    mine = jnp.where(on_chip > 0, mine, lax.ppermute(mine, "yl", swap))
    mine, square = lax.optimization_barrier((mine, square))
    other = lax.ppermute(mine, "core", swap)
    y, x, z = (lax.axis_index(a).astype(I32) for a in TM)
    orders = owners_of_slots(y, x, z, core.astype(I32))
    orders = jnp.concatenate([orders, core.astype(I32)[None]])
    made = products(at, max(SIZES), plan, orders, mine, other, square, design, blocks)
    branches = [functools.partial(rows_of, at, size, blocks) for size in SIZES]
    return lax.switch(choice[0], branches, plan, *made)


def solution(mesh):
    finer = Mesh(mesh.devices.reshape(2, 4, 4, 2, 2), EVERY)
    return jax.shard_map(
        shards,
        mesh=finer,
        in_specs=(P(TM, COL), P(), P(), P()),
        out_specs=P(None, TM, COL),
        check_vma=False,
    )
```
